32 devices in a mesh: blk: 16 (over z, x, core), pair: 2 (over y).
Axes of the slice: x: 2, y: 2, z: 4, core: 2. Of those that a mesh axis runs over, the one named last changes fastest.
Arguments:
- images: bfloat16 [14336, 768], P(('blk', 'pair')), may hold values from -1 to 1
- texts: bfloat16 [14336, 768], P(('blk', 'pair')), may hold values from -1 to 1
- scale: float32 [], replicated, may hold values from 4 to 16
- bias: float32 [], replicated, may hold values from -6 to -2
Outputs:
- row_loss: float32 [14336], P(('blk', 'pair'))
- grad_images: float32 [14336, 768], P(('blk', 'pair'))
- grad_texts: float32 [14336, 768], P(('blk', 'pair'))
The draws below stay inside these ranges and needn't reach their ends.
All inputs are finite; a program needn't handle non-finite values.
Results may differ from the reference program's by a relative error of at most 0.0056.
Values may be sent and summed in bfloat16 or wider, within the bound.
A program may use at most 128 MiB of HBM per device.

```python
import math
import jax
import jax.numpy as jnp
from jax import lax

D = 768
ROWS = 448
STEPS = 6
PAIRS = 14336
N_BLK = 16
N_PAIR = 2


def feature_pair(key):
    subkeys = [jax.random.fold_in(key, 11 + c) for c in range(7)]
    extent = (PAIRS, D)
    shared = jax.random.normal(subkeys[0], extent, jnp.float32)
    noise_picture = jax.random.normal(subkeys[1], extent, jnp.float32)
    noise_caption = jax.random.normal(subkeys[2], extent, jnp.float32)
    columns = jnp.exp(jax.random.uniform(subkeys[3], (1, D), jnp.float32, 0.0, math.log(10.0)))
    rows_picture = jnp.exp(jax.random.uniform(subkeys[4], (PAIRS, 1), jnp.float32, 0.0, math.log(10.0)))
    rows_caption = jnp.exp(jax.random.uniform(subkeys[5], (PAIRS, 1), jnp.float32, 0.0, math.log(10.0)))
    picture = jnp.clip((shared + 0.5 * noise_picture) * columns * rows_picture * 0.004, -1.0, 1.0)
    caption = jnp.clip((0.8 * shared + 0.6 * noise_caption) * columns * rows_caption * 0.004, -1.0, 1.0)
    return (picture, caption)


def draw_images(key, part):
    return feature_pair(key)[0].astype(jnp.bfloat16)


def draw_texts(key, part):
    return feature_pair(key)[1].astype(jnp.bfloat16)


def setup_inputs(seed: int = 0) -> dict:
    arg_keys = jax.random.split(jax.random.key(seed), 5)
    return {
        "images": draw_images(jax.random.fold_in(arg_keys[4], 71), 0),
        "texts": draw_texts(jax.random.fold_in(arg_keys[4], 71), 0),
        "scale": jnp.clip(jnp.exp(jax.random.uniform(arg_keys[2], (), jnp.float32, math.log(4.0), math.log(16.0))), 4.0, 16.0),
        "bias": jnp.clip(jax.random.uniform(arg_keys[3], (), jnp.float32, -6.0, -2.0), -6.0, -2.0),
    }


EPSILON = 1e-06

def unit_rows(features):
    widened = features.astype(jnp.float32)
    inverse = lax.rsqrt(lax.optimization_barrier(jnp.sum(widened * widened, axis=1, keepdims=True)) + EPSILON)
    return (widened * inverse, inverse)

def tangent(unit, inverse, direction):
    return inverse * (direction - unit * lax.optimization_barrier(jnp.sum(unit * direction, axis=1, keepdims=True)))

def reference(images, texts, scale, bias):
    group = N_PAIR * ROWS
    image_unit, image_inverse = unit_rows(images)
    text_unit, text_inverse = unit_rows(texts)
    image_groups = image_unit.astype(jnp.bfloat16).reshape(N_BLK, group, D)
    text_groups = text_unit.astype(jnp.bfloat16).reshape(N_BLK, group, D)
    diagonal = lax.broadcasted_iota(jnp.int32, (group, group), 0) == lax.broadcasted_iota(jnp.int32, (group, group), 1)
    loss_total = jnp.zeros((N_BLK, group), jnp.float32)
    image_dir = jnp.zeros((N_BLK, group, D), jnp.float32)
    text_dir = jnp.zeros((N_BLK, group, D), jnp.float32)
    for offset in range(STEPS):
        shifted = jnp.roll(text_groups, offset, axis=0)
        if offset == 0:
            labels = jnp.where(diagonal, 1.0, -1.0).astype(jnp.float32)
        else:
            labels = jnp.full((group, group), -1.0, jnp.float32)

        def visit_group(operands, labels=labels):
            image_block, text_block = operands
            logits = scale * jnp.dot(image_block, text_block.T, preferred_element_type=jnp.float32) + bias
            margin = labels * logits
            loss_rows = lax.optimization_barrier(jnp.sum(jax.nn.softplus(-margin), axis=1))
            weights_bf = (scale * -labels * jax.nn.sigmoid(-margin)).astype(jnp.bfloat16)
            image_grad = jnp.dot(weights_bf, text_block, preferred_element_type=jnp.float32)
            text_grad = jnp.dot(weights_bf.T, image_block, preferred_element_type=jnp.float32)
            return (loss_rows, image_grad, text_grad)
        loss_rows, image_grad, text_grad = lax.map(visit_group, (image_groups, shifted))
        loss_total = loss_total + loss_rows
        image_dir = image_dir + image_grad
        text_dir = text_dir + jnp.roll(text_grad, -offset, axis=0)
    row_loss = loss_total.reshape(PAIRS) / (STEPS * group)
    grad_images = tangent(image_unit, image_inverse, image_dir.reshape(PAIRS, D))
    grad_texts = tangent(text_unit, text_inverse, text_dir.reshape(PAIRS, D))
    return (row_loss, grad_images, grad_texts)
```

```python
import functools

import jax
import jax.numpy as jnp
from jax import lax
from jax.experimental import pallas as pl
from jax.experimental.pallas import tpu as pltpu
from jax.sharding import PartitionSpec as P

STEPS = 6
EPSILON = 1e-06
MESH = pl.DeviceIdType.MESH

OWN, FAR, NEAR, FAR_SIB, NEAR_SIB, LAST = range(6)
S_FAR, S_NEAR, S_OWN_SIB, S_FAR_SIB, S_NEAR_SIB, S_LAST = range(6)


def unit_rows(features):
    widened = features.astype(jnp.float32)
    inverse = lax.rsqrt(jnp.sum(widened * widened, axis=1, keepdims=True) + EPSILON)
    return (widened * inverse, inverse)


def tangent(unit, inverse, direction):
    return inverse * (direction - unit * jnp.sum(unit * direction, axis=1, keepdims=True))


def kernel(
    n_blk,
    images_ref,
    texts_ref,
    scale_ref,
    bias_ref,
    loss_out,
    grad_images,
    grad_texts,
    keys,
    part,
    acc,
    out_part,
    in_part,
    loss_acc,
    loss_send,
    loss_recv,
    send_sem,
    recv_sem,
    part_sem,
    sum_sem,
    loss_sem,
):
    rows, width = images_ref.shape
    chunk = rows // 2
    me = lax.axis_index("blk")
    pair = lax.axis_index("pair")
    other = 1 - pair
    xpartner = jnp.where(lax.rem(me // 2, 2) == 0, me + 2, me - 2)

    def wrap(position):
        return lax.rem(position + n_blk, n_blk)

    barrier = pltpu.get_barrier_semaphore()
    peers = [(wrap(me + d), pair) for d in (-4, -3, -1, 1, 3, 4)]
    peers += [(xpartner, pair), (me, other)]
    for peer in peers:
        pl.semaphore_signal(barrier, inc=1, device_id=peer, device_id_type=MESH)

    scale = scale_ref[0]
    bias = bias_ref[0]

    text_unit, _ = unit_rows(texts_ref[...])
    keys[0, OWN] = text_unit.astype(jnp.bfloat16)
    image_unit, _ = unit_rows(images_ref[...])
    keys[1, OWN] = image_unit.astype(jnp.bfloat16)
    pl.semaphore_wait(barrier, len(peers))

    def place(side):
        return me if side == 0 else n_blk - 1 - me

    def device(side, position):
        position = wrap(position)
        return (position if side == 0 else n_blk - 1 - position, pair)

    def block_copy(side, send, source, target, c, dst):
        span = pl.ds(c * chunk, chunk)
        return pltpu.make_async_remote_copy(
            src_ref=keys.at[side, source, span],
            dst_ref=keys.at[side, target, span],
            send_sem=send_sem.at[side, send, c],
            recv_sem=recv_sem.at[side, target, c],
            device_id=dst,
            device_id_type=MESH,
        )

    def far(side, c):
        return block_copy(side, S_FAR, OWN, FAR, c, device(side, place(side) + 4))

    def near(side, c, source):
        return block_copy(side, S_NEAR, source, NEAR, c, (xpartner, pair))

    def own_sib(side, c):
        return block_copy(side, S_OWN_SIB, OWN, LAST, c, device(side, place(side) + 1))

    def sib(side, send, source, target, c):
        position = place(side)
        core = lax.rem(position, 2)
        return block_copy(side, send, source, target, c, device(side, position + 1 - 2 * core))

    def last(side, c, source):
        step = 1 if source == FAR else 3
        send = S_LAST if source == FAR else S_OWN_SIB
        return block_copy(side, send, source, LAST, c, device(side, place(side) + step))

    def roles(side):
        position = place(side)
        even_chip = lax.rem(position // 2, 2) == 0
        first_core = lax.rem(position, 2) == 0
        return even_chip, first_core

    part_copies = []
    for side in (0, 1):
        part_copies.append(
            pltpu.make_async_remote_copy(
                src_ref=keys.at[1 - side, OWN],
                dst_ref=part.at[side],
                send_sem=part_sem.at[0, side],
                recv_sem=part_sem.at[1, side],
                device_id=(me, other),
                device_id_type=MESH,
            )
        )

    for side in (0, 1):
        even_chip, first_core = roles(side)
        for c in (0, 1):
            far(side, c).start()

            @pl.when(even_chip)
            def _():
                near(side, c, OWN).start()

        part_copies[side].start()

        @pl.when(first_core)
        def _():
            for c in (0, 1):
                own_sib(side, c).start()

    def after_far(side):
        even_chip, first_core = roles(side)
        for c in (0, 1):
            far(side, c).wait_recv()

            @pl.when(jnp.logical_not(even_chip))
            def _():
                near(side, c, FAR).start()

            @pl.when(jnp.logical_and(even_chip, jnp.logical_not(first_core)))
            def _():
                last(side, c, FAR).start()

            sib(side, S_FAR_SIB, FAR, FAR_SIB, c).start()

    def after_near(side):
        even_chip, first_core = roles(side)
        for c in (0, 1):
            near(side, c, OWN).wait_recv()

            @pl.when(jnp.logical_and(even_chip, jnp.logical_not(first_core)))
            def _():
                last(side, c, NEAR).start()

            sib(side, S_NEAR_SIB, NEAR, NEAR_SIB, c).start()

    def wait_block(side, slot):
        for c in (0, 1):
            own_like = block_copy(side, S_FAR, OWN, slot, c, (me, other))
            own_like.wait_recv()

    acc[...] = jnp.zeros_like(acc)
    loss_acc[...] = jnp.zeros_like(loss_acc)

    def tile(side, half, slot, diagonal):
        query = keys.at[1 - side, OWN] if half == 0 else part.at[side]
        key = keys[side, slot]
        for c in range(2):
            span = pl.ds(c * chunk, chunk)
            dots = lax.dot_general(
                query[span, :], key, (((1,), (1,)), ((), ())), preferred_element_type=jnp.float32
            )
            value = scale * dots + bias
            if diagonal:
                row = lax.broadcasted_iota(jnp.int32, dots.shape, 0) + c * chunk
                column = lax.broadcasted_iota(jnp.int32, dots.shape, 1)
                sign = jnp.where(row == column, -1.0, 1.0)
                value = sign * value
                gain = sign * scale
            else:
                gain = scale
            grown = jnp.exp(value)
            total = 1.0 + grown
            weights = (gain * (grown / total)).astype(jnp.bfloat16)
            acc[side, half, span, :] += jnp.dot(weights, key, preferred_element_type=jnp.float32)
            if side == 0:
                loss = jnp.where(grown < 2.0**-11, grown, jnp.log(total))
                loss_acc[half, span, :] += jnp.broadcast_to(
                    jnp.sum(loss, axis=1, keepdims=True), (chunk, 128)
                )

    sum_copies = []
    for side in (0, 1):
        sum_copies.append(
            pltpu.make_async_remote_copy(
                src_ref=out_part.at[side],
                dst_ref=in_part.at[side],
                send_sem=sum_sem.at[0, side],
                recv_sem=sum_sem.at[1, side],
                device_id=(me, other),
                device_id_type=MESH,
            )
        )
    loss_copy = pltpu.make_async_remote_copy(
        src_ref=loss_send,
        dst_ref=loss_recv,
        send_sem=loss_sem.at[0],
        recv_sem=loss_sem.at[1],
        device_id=(me, other),
        device_id_type=MESH,
    )

    def send_part(side):
        out_part[side] = acc[side, 1].astype(jnp.bfloat16)
        sum_copies[side].start()

    tile(0, 0, OWN, True)
    tile(1, 0, OWN, True)
    after_far(0)
    tile(0, 0, FAR, False)
    after_far(1)
    tile(1, 0, FAR, False)
    part_copies[0].wait_recv()
    after_near(0)

    def both(side, slot):
        tile(side, 1, slot, False)
        tile(side, 0, slot, False)

    tile(0, 1, OWN, False)
    tile(0, 1, FAR, False)
    after_near(1)
    part_copies[1].wait_recv()
    both(0, NEAR)
    tile(1, 1, OWN, False)
    tile(1, 1, FAR, False)
    both(1, NEAR)

    def rest(side):
        @pl.loop(FAR_SIB, LAST + 1)
        def _(slot):
            wait_block(side, slot)
            tile(side, 1, slot, False)

        send_part(side)
        if side == 0:
            loss_send[...] = jnp.transpose(loss_acc[1])[:8, :]
            loss_copy.start()

        @pl.loop(FAR_SIB, LAST + 1)
        def _(slot):
            tile(side, 0, slot, False)

    rest(0)
    rest(1)

    def finish(side, features, out):
        sum_copies[side].wait_recv()
        for c in range(2):
            span = pl.ds(c * chunk, chunk)
            unit, inverse = unit_rows(features[span, :])
            direction = acc[side, 0, span, :] + in_part[side, span, :].astype(jnp.float32)
            out[span, :] = tangent(unit, inverse, direction)

    finish(0, images_ref, grad_images)
    loss_copy.wait_recv()
    window = STEPS * 2 * rows
    loss_out[...] = (jnp.transpose(loss_acc[0])[:8, :] + loss_recv[...]) / window
    finish(1, texts_ref, grad_texts)

    for side in (0, 1):
        even_chip, first_core = roles(side)
        part_copies[side].wait_send()
        sum_copies[side].wait_send()
        for c in (0, 1):
            far(side, c).wait_send()
            near(side, c, OWN).wait_send()
            sib(side, S_FAR_SIB, FAR, FAR_SIB, c).wait_send()
            sib(side, S_NEAR_SIB, NEAR, NEAR_SIB, c).wait_send()

            @pl.when(first_core)
            def _():
                own_sib(side, c).wait_send()

            @pl.when(jnp.logical_and(even_chip, jnp.logical_not(first_core)))
            def _():
                last(side, c, FAR).wait_send()
                last(side, c, NEAR).wait_send()

    loss_copy.wait_send()


def body(n_blk, images, texts, scale, bias):
    rows, width = images.shape
    vmem = pl.BlockSpec(memory_space=pltpu.VMEM)
    smem = pl.BlockSpec(memory_space=pltpu.SMEM)
    loss, grad_images, grad_texts = pl.pallas_call(
        functools.partial(kernel, n_blk),
        out_shape=(
            jax.ShapeDtypeStruct((8, rows), jnp.float32),
            jax.ShapeDtypeStruct((rows, width), jnp.float32),
            jax.ShapeDtypeStruct((rows, width), jnp.float32),
        ),
        in_specs=[vmem, vmem, smem, smem],
        out_specs=(vmem, vmem, vmem),
        scratch_shapes=[
            pltpu.VMEM((2, STEPS, rows, width), jnp.bfloat16),
            pltpu.VMEM((2, rows, width), jnp.bfloat16),
            pltpu.VMEM((2, 2, rows, width), jnp.float32),
            pltpu.VMEM((2, rows, width), jnp.bfloat16),
            pltpu.VMEM((2, rows, width), jnp.bfloat16),
            pltpu.VMEM((2, rows, 128), jnp.float32),
            pltpu.VMEM((8, rows), jnp.float32),
            pltpu.VMEM((8, rows), jnp.float32),
            pltpu.SemaphoreType.DMA((2, 6, 2)),
            pltpu.SemaphoreType.DMA((2, 6, 2)),
            pltpu.SemaphoreType.DMA((2, 2)),
            pltpu.SemaphoreType.DMA((2, 2)),
            pltpu.SemaphoreType.DMA((2,)),
        ],
        compiler_params=pltpu.CompilerParams(
            collective_id=0, has_side_effects=True, vmem_limit_bytes=56 * 1024 * 1024
        ),
    )(images, texts, scale.reshape(1), bias.reshape(1))
    return (loss[0], grad_images, grad_texts)


def solution(mesh):
    in_specs = (P(("blk", "pair"), None), P(("blk", "pair"), None), P(), P())
    out_specs = (P(("blk", "pair")), P(("blk", "pair"), None), P(("blk", "pair"), None))
    return jax.shard_map(
        functools.partial(body, mesh.shape["blk"]),
        mesh=mesh,
        in_specs=in_specs,
        out_specs=out_specs,
        check_vma=False,
    )
```

```python
import functools

import jax
import jax.numpy as jnp
from jax import lax
from jax.experimental import pallas as pl
from jax.experimental.pallas import tpu as pltpu
from jax.sharding import PartitionSpec as P

STEPS = 6
EPSILON = 1e-06
MESH = pl.DeviceIdType.MESH

OWN, FAR, NEAR, FAR_SIB, NEAR_SIB, LAST = range(6)
S_FAR, S_NEAR, S_OWN_SIB, S_FAR_SIB, S_NEAR_SIB, S_LAST = range(6)


def unit_rows(features):
    widened = features.astype(jnp.float32)
    inverse = lax.rsqrt(jnp.sum(widened * widened, axis=1, keepdims=True) + EPSILON)
    return (widened * inverse, inverse)


def tangent(unit, inverse, direction):
    return inverse * (direction - unit * jnp.sum(unit * direction, axis=1, keepdims=True))


R_FAR, R_NEAR, R_OWN, R_LAST_FAR, R_LAST_NEAR, R_X, R_DONE = range(7)
O_FAR_SIB, O_NEAR_SIB, O_LAST, O_NEAR, O_FAR = range(5)


def kernel(
    n_blk,
    images_ref,
    texts_ref,
    scale_ref,
    bias_ref,
    loss_out,
    grad_images,
    grad_texts,
    keys,
    query_own,
    query_other,
    acc,
    text_acc,
    leave,
    back,
    out_part,
    in_part,
    loss_acc,
    loss_send,
    loss_recv,
    send_sem,
    recv_sem,
    leave_sem,
    back_sem,
    part_sem,
    sum_sem,
    loss_sem,
):
    rows, width = images_ref.shape
    chunk = rows // 2
    me = lax.axis_index("blk")
    pair = lax.axis_index("pair")
    other = 1 - pair
    even_chip = lax.rem(me // 2, 2) == 0
    odd_chip = jnp.logical_not(even_chip)
    first_core = lax.rem(me, 2) == 0
    second_core = jnp.logical_not(first_core)
    relay = jnp.logical_and(even_chip, second_core)
    xpartner = (jnp.where(even_chip, me + 2, me - 2), pair)
    sibling = (me + 1 - 2 * lax.rem(me, 2), pair)

    def at(distance):
        return (lax.rem(me + distance + n_blk, n_blk), pair)

    barrier = pltpu.get_barrier_semaphore()
    peers = [at(d) for d in (-4, -3, -1, 1, 3, 4)] + [xpartner, (me, other)]
    for peer in peers:
        pl.semaphore_signal(barrier, inc=1, device_id=peer, device_id_type=MESH)

    scale = scale_ref[0]
    bias = bias_ref[0]
    keys[OWN] = unit_rows(texts_ref[...])[0].astype(jnp.bfloat16)
    query_own[...] = unit_rows(images_ref[...])[0].astype(jnp.bfloat16)
    pl.semaphore_wait(barrier, len(peers))

    def key_copy(send, source, target, c, dst):
        span = pl.ds(c * chunk, chunk)
        return pltpu.make_async_remote_copy(
            src_ref=keys.at[source, span],
            dst_ref=keys.at[target, span],
            send_sem=send_sem.at[send, c],
            recv_sem=recv_sem.at[target, c],
            device_id=dst,
            device_id_type=MESH,
        )

    def far(c):
        return key_copy(S_FAR, OWN, FAR, c, at(4))

    def near(c, source):
        return key_copy(S_NEAR, source, NEAR, c, xpartner)

    def own_sib(c):
        return key_copy(S_OWN_SIB, OWN, LAST, c, sibling)

    def far_sib(c):
        return key_copy(S_FAR_SIB, FAR, FAR_SIB, c, sibling)

    def near_sib(c):
        return key_copy(S_NEAR_SIB, NEAR, NEAR_SIB, c, sibling)

    def last_far(c):
        return key_copy(S_LAST, FAR, LAST, c, at(1))

    def last_near(c):
        return key_copy(S_OWN_SIB, NEAR, LAST, c, at(3))

    def sum_copy(source, target, c, dst):
        span = pl.ds(c * chunk, chunk)
        return pltpu.make_async_remote_copy(
            src_ref=leave.at[source, span],
            dst_ref=back.at[target, span],
            send_sem=leave_sem.at[source, c],
            recv_sem=back_sem.at[target, c],
            device_id=dst,
            device_id_type=MESH,
        )

    part_copy = pltpu.make_async_remote_copy(
        src_ref=query_own,
        dst_ref=query_other,
        send_sem=part_sem.at[0],
        recv_sem=part_sem.at[1],
        device_id=(me, other),
        device_id_type=MESH,
    )
    part_sum = pltpu.make_async_remote_copy(
        src_ref=out_part,
        dst_ref=in_part,
        send_sem=sum_sem.at[0],
        recv_sem=sum_sem.at[1],
        device_id=(me, other),
        device_id_type=MESH,
    )
    loss_copy = pltpu.make_async_remote_copy(
        src_ref=loss_send,
        dst_ref=loss_recv,
        send_sem=loss_sem.at[0],
        recv_sem=loss_sem.at[1],
        device_id=(me, other),
        device_id_type=MESH,
    )

    part_copy.start()
    for c in (0, 1):
        far(c).start()

        @pl.when(even_chip)
        def _():
            near(c, OWN).start()

    @pl.when(first_core)
    def _():
        for c in (0, 1):
            own_sib(c).start()

    def after_far(c):
        far(c).wait_recv()

        @pl.when(odd_chip)
        def _():
            near(c, FAR).start()

        @pl.when(relay)
        def _():
            last_far(c).start()

        far_sib(c).start()

    def after_near(c):
        near(c, OWN).wait_recv()

        @pl.when(relay)
        def _():
            last_near(c).start()

        near_sib(c).start()

    acc[...] = jnp.zeros_like(acc)
    loss_acc[...] = jnp.zeros_like(loss_acc)

    def tile(half, slot, diagonal=False, fresh=False):
        query = query_own if half == 0 else query_other
        key = keys[slot]
        pieces = []
        for c in range(2):
            span = pl.ds(c * chunk, chunk)
            dots = lax.dot_general(
                query[span, :], key, (((1,), (1,)), ((), ())), preferred_element_type=jnp.float32
            )
            value = scale * dots + bias
            gain = scale
            if diagonal:
                row = lax.broadcasted_iota(jnp.int32, dots.shape, 0) + c * chunk
                column = lax.broadcasted_iota(jnp.int32, dots.shape, 1)
                sign = jnp.where(row == column, -1.0, 1.0)
                value = sign * value
                gain = sign * scale
            grown = jnp.exp(value)
            total = 1.0 + grown
            weights = (gain * (grown / total)).astype(jnp.bfloat16)
            pieces.append(weights)
            acc[half, span, :] += jnp.dot(weights, key, preferred_element_type=jnp.float32)
            loss = jnp.where(grown < 2.0**-11, grown, jnp.log(total))
            loss_acc[half, span, :] += jnp.broadcast_to(
                jnp.sum(loss, axis=1, keepdims=True), (chunk, 128)
            )
        text_term = lax.dot_general(
            jnp.concatenate(pieces, axis=0),
            query[...],
            (((0,), (0,)), ((), ())),
            preferred_element_type=jnp.float32,
        )
        if fresh:
            text_acc[slot] = text_term
        else:
            text_acc[slot] += text_term

    def both(slot):
        tile(1, slot, fresh=True)
        tile(0, slot)

    def depart(slot, source, c):
        span = pl.ds(c * chunk, chunk)
        leave[source, span, :] = text_acc[slot, span, :].astype(jnp.bfloat16)

    def term(target, c):
        return back[target, pl.ds(c * chunk, chunk), :].astype(jnp.float32)

    tile(0, OWN, diagonal=True, fresh=True)
    after_far(0)
    after_far(1)
    tile(0, FAR, fresh=True)
    part_copy.wait_recv()
    tile(1, OWN)
    after_near(0)
    after_near(1)
    tile(1, FAR)

    def wait_keys(slot):
        for c in (0, 1):
            key_copy(S_FAR, OWN, slot, c, sibling).wait_recv()

    wait_keys(FAR_SIB)
    both(FAR_SIB)
    for c in (0, 1):
        depart(FAR_SIB, O_FAR_SIB, c)
        sum_copy(O_FAR_SIB, R_FAR, c, sibling).start()
    wait_keys(NEAR_SIB)
    both(NEAR_SIB)
    for c in (0, 1):
        depart(NEAR_SIB, O_NEAR_SIB, c)
        sum_copy(O_NEAR_SIB, R_NEAR, c, sibling).start()
    both(NEAR)

    def pass_on(slot, source, target, dst, arrivals, c):
        span = pl.ds(c * chunk, chunk)
        total = text_acc[slot, span, :]
        for arrival in arrivals:
            sum_copy(source, arrival, c, sibling).wait_recv()
            total += term(arrival, c)
        leave[source, span, :] = total.astype(jnp.bfloat16)
        sum_copy(source, target, c, dst).start()

    def send_near(c, arrivals):
        pass_on(NEAR, O_NEAR, R_X, xpartner, arrivals, c)

    def send_far(c, arrivals):
        pass_on(FAR, O_FAR, R_DONE, at(-4), arrivals, c)

    free = jnp.logical_not(relay)
    early = jnp.logical_and(even_chip, first_core)

    @pl.when(free)
    def _():
        for c in (0, 1):
            send_near(c, (R_NEAR,))

    @pl.when(early)
    def _():
        for c in (0, 1):
            send_far(c, (R_FAR,))

    wait_keys(LAST)
    both(LAST)
    for c in (0, 1):
        depart(LAST, O_LAST, c)

        @pl.when(second_core)
        def _():
            sum_copy(O_LAST, R_OWN, c, sibling).start()

        @pl.when(jnp.logical_and(first_core, odd_chip))
        def _():
            sum_copy(O_LAST, R_LAST_FAR, c, at(-1)).start()

        @pl.when(early)
        def _():
            sum_copy(O_LAST, R_LAST_NEAR, c, at(-3)).start()

    out_part[...] = acc[1].astype(jnp.bfloat16)
    part_sum.start()
    loss_send[...] = jnp.transpose(loss_acc[1])[:8, :]
    loss_copy.start()

    for c in (0, 1):

        @pl.when(relay)
        def _():
            send_near(c, (R_NEAR, R_LAST_NEAR))

    for c in (0, 1):

        @pl.when(odd_chip)
        def _():
            send_far(c, (R_FAR, R_X))

        @pl.when(relay)
        def _():
            send_far(c, (R_FAR, R_LAST_FAR))

    part_sum.wait_recv()
    for c in (0, 1):
        span = pl.ds(c * chunk, chunk)
        unit, inverse = unit_rows(images_ref[span, :])
        direction = acc[0, span, :] + in_part[span, :].astype(jnp.float32)
        grad_images[span, :] = tangent(unit, inverse, direction)
    loss_copy.wait_recv()
    window = STEPS * 2 * rows
    loss_out[...] = (jnp.transpose(loss_acc[0])[:8, :] + loss_recv[...]) / window

    for c in (0, 1):
        span = pl.ds(c * chunk, chunk)

        @pl.when(first_core)
        def _():
            sum_copy(O_LAST, R_OWN, c, sibling).wait_recv()
            text_acc[OWN, span, :] += term(R_OWN, c)

        @pl.when(even_chip)
        def _():
            sum_copy(O_NEAR, R_X, c, xpartner).wait_recv()
            text_acc[OWN, span, :] += term(R_X, c)

        sum_copy(O_FAR, R_DONE, c, at(-4)).wait_recv()
        unit, inverse = unit_rows(texts_ref[span, :])
        direction = text_acc[OWN, span, :] + term(R_DONE, c)
        grad_texts[span, :] = tangent(unit, inverse, direction)

    part_copy.wait_send()
    part_sum.wait_send()
    loss_copy.wait_send()
    for c in (0, 1):
        far(c).wait_send()
        near(c, OWN).wait_send()
        far_sib(c).wait_send()
        near_sib(c).wait_send()
        for source in (O_FAR_SIB, O_NEAR_SIB, O_LAST, O_NEAR, O_FAR):
            sum_copy(source, R_FAR, c, sibling).wait_send()

        @pl.when(first_core)
        def _():
            own_sib(c).wait_send()

        @pl.when(relay)
        def _():
            last_far(c).wait_send()
            last_near(c).wait_send()


def body(n_blk, images, texts, scale, bias):
    rows, width = images.shape
    vmem = pl.BlockSpec(memory_space=pltpu.VMEM)
    smem = pl.BlockSpec(memory_space=pltpu.SMEM)
    loss, grad_images, grad_texts = pl.pallas_call(
        functools.partial(kernel, n_blk),
        out_shape=(
            jax.ShapeDtypeStruct((8, rows), jnp.float32),
            jax.ShapeDtypeStruct((rows, width), jnp.float32),
            jax.ShapeDtypeStruct((rows, width), jnp.float32),
        ),
        in_specs=[vmem, vmem, smem, smem],
        out_specs=(vmem, vmem, vmem),
        scratch_shapes=[
            pltpu.VMEM((STEPS, rows, width), jnp.bfloat16),
            pltpu.VMEM((rows, width), jnp.bfloat16),
            pltpu.VMEM((rows, width), jnp.bfloat16),
            pltpu.VMEM((2, rows, width), jnp.float32),
            pltpu.VMEM((STEPS, rows, width), jnp.float32),
            pltpu.VMEM((5, rows, width), jnp.bfloat16),
            pltpu.VMEM((7, rows, width), jnp.bfloat16),
            pltpu.VMEM((rows, width), jnp.bfloat16),
            pltpu.VMEM((rows, width), jnp.bfloat16),
            pltpu.VMEM((2, rows, 128), jnp.float32),
            pltpu.VMEM((8, rows), jnp.float32),
            pltpu.VMEM((8, rows), jnp.float32),
            pltpu.SemaphoreType.DMA((6, 2)),
            pltpu.SemaphoreType.DMA((6, 2)),
            pltpu.SemaphoreType.DMA((5, 2)),
            pltpu.SemaphoreType.DMA((7, 2)),
            pltpu.SemaphoreType.DMA((2,)),
            pltpu.SemaphoreType.DMA((2,)),
            pltpu.SemaphoreType.DMA((2,)),
        ],
        compiler_params=pltpu.CompilerParams(
            collective_id=0, has_side_effects=True, vmem_limit_bytes=56 * 1024 * 1024
        ),
    )(images, texts, scale.reshape(1), bias.reshape(1))
    return (loss[0], grad_images, grad_texts)


def solution(mesh):
    in_specs = (P(("blk", "pair"), None), P(("blk", "pair"), None), P(), P())
    out_specs = (P(("blk", "pair")), P(("blk", "pair"), None), P(("blk", "pair"), None))
    return jax.shard_map(
        functools.partial(body, mesh.shape["blk"]),
        mesh=mesh,
        in_specs=in_specs,
        out_specs=out_specs,
        check_vma=False,
    )
```
